512 devices in a mesh: grp: 16 (over y_hi, z), seq: 32 (over x, y_lo, core).
Axes of the slice: x: 4, y: 8 (y_hi: 2, y_lo: 4; y = y_hi * 4 + y_lo), z: 8, core: 2. Of those that a mesh axis runs over, the one named last changes fastest.
Arguments:
- text_heads: bfloat16 [16, 512, 3, 2048], P('grp', 'seq'), may hold values from -6 to 6
- image_heads: bfloat16 [16, 2048, 3, 2048], P('grp', 'seq'), may hold values from -6 to 6
- text_cotangent: bfloat16 [16, 512, 2048], P('grp', 'seq'), may hold values from -3 to 3
- image_cotangent: bfloat16 [16, 2048, 2048], P('grp', 'seq'), may hold values from -3 to 3
- control_residual: bfloat16 [16, 32, 64, 2048], P(None, 'seq', 'grp'), may hold values from -1.5 to 1.5
- control_gain: float32 [2048], replicated, may hold values from 0.1 to 1.9
- text_lengths: int32 [16], P('grp'), may hold values from 64 to 512, as said below
Outputs:
- text_attention: bfloat16 [16, 512, 2048], P('grp', 'seq')
- image_output: bfloat16 [16, 2048, 2048], P('grp', 'seq')
- text_grads: bfloat16 [16, 512, 3, 2048], P('grp', 'seq')
- image_grads: bfloat16 [16, 2048, 3, 2048], P('grp', 'seq')
- control_grads: bfloat16 [16, 32, 64, 2048], P(None, 'seq', 'grp')
The draws below stay inside these ranges and needn't reach their ends.
Inputs may be any that keep to these rules, and one draw needn't show every extreme that they name: `text_lengths`: padding text tokens follow the valid ones.
All inputs are finite; a program needn't handle non-finite values.
Results may differ from the reference program's by a relative error of at most 0.033.
Values may be sent and summed in bfloat16 or wider, within the bound.
No kernel may reach another device: no remote copies, remote signals or barrier semaphores. Data moves between devices by JAX's collectives and lax.ppermute only.
A program may use at most 64 MiB of HBM per device.

```python
import math
import jax
import jax.numpy as jnp
from jax import lax

HEADS = 16
HEAD_DIM = 128
IMG_DEV = 64
HD = 2048
IMAGES = 16
L_TXT = 512
L_IMG = 2048
SEQ_BLOCKS = 32


def draw_image_heads(key, part):
    key = jax.random.fold_in(key, 11)
    full_shape = (IMAGES, L_IMG, 3, HEADS * HEAD_DIM)
    result = jnp.clip(jax.random.normal(key, full_shape, jnp.float32), -6.0, 6.0)
    return result.astype(jnp.bfloat16)


def draw_text_lengths(key, part):
    key = jax.random.fold_in(key, 23)
    lengths = jax.random.randint(key, (IMAGES,), L_TXT // 8, L_TXT + 1)
    longest = jax.random.randint(jax.random.fold_in(key, 1), (), 0, IMAGES)
    offset = jax.random.randint(jax.random.fold_in(key, 2), (), 0, IMAGES - 1)
    shortest = (longest + 1 + offset) % IMAGES
    image_ids = jnp.arange(IMAGES, dtype=jnp.int32)
    lengths = jnp.where(image_ids == longest, L_TXT, lengths)
    lengths = jnp.where(image_ids == shortest, L_TXT // 8, lengths)
    return lengths.astype(jnp.int32)


def levels(stream_key, dims, cuts, smallest, high):
    def one(axis_at, blocks):
        heights = jax.random.uniform(jax.random.fold_in(jax.random.fold_in(stream_key, 6), axis_at), (blocks,), jnp.float32, smallest / len(cuts), high / len(cuts))
        return jnp.repeat(jnp.exp(heights), dims[axis_at] // blocks).reshape((-1,) + (1,) * (len(dims) - axis_at - 1))

    loudness = one(*cuts[0])
    for cut in cuts[1:]:
        loudness = loudness * one(*cut)
    return loudness


def centred(stream_key, dims, deviation, bound, cuts=(), kind=jnp.bfloat16):
    entries = jax.random.normal(stream_key, dims, jnp.float32) * deviation
    if len(cuts) > 0:
        entries = levels(stream_key, dims, cuts, -0.22, 0.18) * entries
    return jnp.clip(entries, min=-bound, max=bound).astype(kind)


def setup_inputs(seed: int = 0) -> dict:
    seeds = jax.random.split(jax.random.key(seed), 8)
    return {
        "text_heads": centred(seeds[0], (IMAGES, L_TXT, 3, HD), 1.0, 6.0, ((0, 16), (1, 32))),
        "image_heads": draw_image_heads(jax.random.fold_in(seeds[7], 71), 0),
        "text_cotangent": centred(seeds[2], (IMAGES, L_TXT, HD), 0.5, 3.0, ((0, 16), (1, 32))),
        "image_cotangent": centred(seeds[3], (IMAGES, L_IMG, HD), 0.5, 3.0, ((0, 16), (1, 32))),
        "control_residual": centred(seeds[4], (IMAGES, SEQ_BLOCKS, IMG_DEV, HD), 0.25, 1.5, ((1, 32), (2, 16))),
        "control_gain": jnp.clip(1.0 + 0.18 * jax.random.normal(seeds[5], (HD,), jnp.float32), 0.1, 1.9),
        "text_lengths": draw_text_lengths(jax.random.fold_in(seeds[7], 71), 0),
    }


def head_pass(queries, keys_in, values_in, upstream, valid):
    scale_factor = 1.0 / math.sqrt(HEAD_DIM)
    scores = jnp.dot(queries, keys_in.T, preferred_element_type=jnp.float32) * scale_factor
    scores = jnp.where(valid[None, :], scores, -jnp.inf)
    row_max = lax.optimization_barrier(jnp.max(scores, axis=1, keepdims=True))
    shifted = jnp.exp(scores - row_max)
    probs = shifted / lax.optimization_barrier(jnp.sum(shifted, axis=1, keepdims=True))
    weights = probs.astype(jnp.bfloat16)
    attention = jnp.dot(weights, values_in, preferred_element_type=jnp.float32).astype(jnp.bfloat16)
    delta = lax.optimization_barrier(jnp.sum(upstream.astype(jnp.float32) * attention.astype(jnp.float32), axis=1, keepdims=True))
    value_grad = jnp.dot(weights.T, upstream, preferred_element_type=jnp.float32).astype(jnp.bfloat16)
    prob_grad = jnp.dot(upstream, values_in.T, preferred_element_type=jnp.float32)
    score_grad = (probs * (prob_grad - delta)).astype(jnp.bfloat16)
    query_grad = (jnp.dot(score_grad, keys_in, preferred_element_type=jnp.float32) * scale_factor).astype(jnp.bfloat16)
    key_grad = (jnp.dot(score_grad.T, queries, preferred_element_type=jnp.float32) * scale_factor).astype(jnp.bfloat16)
    return (attention, query_grad, key_grad, value_grad)

def image_pass(items):
    text_block, image_block, text_up, image_up, length = items
    joint = jnp.concatenate([text_block, image_block], axis=0)
    total_rows = joint.shape[0]
    joint = joint.reshape(total_rows, 3, HEADS, HEAD_DIM)
    upstream = jnp.concatenate([text_up, image_up], axis=0).reshape(total_rows, HEADS, HEAD_DIM)
    positions = jnp.arange(total_rows, dtype=jnp.int32)
    valid = (positions >= L_TXT) | (positions < length)

    def one_head(head_items):
        block, grads_in = head_items
        return head_pass(block[:, 0], block[:, 1], block[:, 2], grads_in, valid)
    attention, query_grad, key_grad, value_grad = lax.map(one_head, (jnp.moveaxis(joint, 2, 0), jnp.moveaxis(upstream, 1, 0)))
    attention = jnp.moveaxis(attention, 0, 1).reshape(total_rows, HEADS * HEAD_DIM)
    grads_all = jnp.stack([query_grad, key_grad, value_grad], axis=2)
    grads_all = jnp.moveaxis(grads_all, 0, 2).reshape(total_rows, 3, HEADS * HEAD_DIM)
    return (attention, grads_all)

def reference(text_heads, image_heads, text_cotangent, image_cotangent, control_residual, control_gain, text_lengths):
    attention, grads_all = lax.map(image_pass, (text_heads, image_heads, text_cotangent, image_cotangent, text_lengths))
    residual = control_residual.reshape(IMAGES, L_IMG, HEADS * HEAD_DIM).astype(jnp.float32)
    text_attention = attention[:, :L_TXT]
    image_output = (attention[:, L_TXT:].astype(jnp.float32) + control_gain * residual).astype(jnp.bfloat16)
    control_grads = (control_gain * image_cotangent.astype(jnp.float32)).astype(jnp.bfloat16).reshape(control_residual.shape)
    return (text_attention, image_output, grads_all[:, :L_TXT], grads_all[:, L_TXT:], control_grads)
```

```python
import functools
import math

import jax
import jax.numpy as jnp
from jax import lax
from jax.experimental import pallas as pl
from jax.experimental.pallas import tpu as pltpu
from jax.sharding import Mesh, PartitionSpec as P

HEAD = 128
HEADS = 16
TXT = 16
IMG = 64
ROWS = TXT + IMG
CHIPS = 16
SCALE = 1.0 / math.sqrt(HEAD)
SCALE2 = SCALE * math.log2(math.e)
BQ = 256
BK = 512
NQ = CHIPS * ROWS
NK = 2 * NQ
TXT_KEYS = 2 * CHIPS * TXT

VM = pl.BlockSpec(memory_space=pltpu.VMEM)
SM = pl.BlockSpec(memory_space=pltpu.SMEM)


def dot(a, b):
    return lax.dot_general(a, b, (((1,), (0,)), ((), ())), preferred_element_type=jnp.float32)


def dot_t(a, b):
    return lax.dot_general(a, b, (((1,), (1,)), ((), ())), preferred_element_type=jnp.float32)


def pack_kernel(th, ih, tc, ic, out):
    for h in range(HEADS):
        cols = slice(h * HEAD, (h + 1) * HEAD)
        for t in range(3):
            out[h, t, :TXT, :] = th[t, :, cols]
            out[h, t, TXT:, :] = ih[t, :, cols]
        out[h, 3, :TXT, :] = tc[:, cols]
        out[h, 3, TXT:, :] = ic[:, cols]


def attention_kernel(
    info, own, oth, aq, part_own, part_oth, q_s, g_s, k_s, v_s, s_s, e_s, dk_s, dv_s, mask_s
):
    length = info[0]
    core = info[1]
    half_txt = CHIPS * TXT
    half_img = CHIPS * IMG
    for s in range(CHIPS):
        q_s[s * ROWS : (s + 1) * ROWS, :] = own[s, 0]
        g_s[s * ROWS : (s + 1) * ROWS, :] = own[s, 3]
        for h, src in ((0, own), (1, oth)):
            for t, dst in ((1, k_s), (2, v_s)):
                at = h * half_txt + s * TXT
                dst[at : at + TXT, :] = src[s, t, :TXT, :]
                at = TXT_KEYS + h * half_img + s * IMG
                dst[at : at + IMG, :] = src[s, t, TXT:, :]
    pos = lax.broadcasted_iota(jnp.int32, (8, TXT_KEYS), 1)
    half = jnp.where(pos < half_txt, core, 1 - core)
    token = ((pos % half_txt) // TXT) * (2 * TXT) + half * TXT + pos % TXT
    mask_s[...] = jnp.where(token < length, 0.0, -jnp.inf)
    dk_s[...] = jnp.zeros_like(dk_s)
    dv_s[...] = jnp.zeros_like(dv_s)
    chunks = NK // BK

    def block(i):
        rows = slice(i * BQ, (i + 1) * BQ)
        q = q_s[rows, :]
        g = g_s[rows, :]
        top = jnp.full((BQ, 128), -jnp.inf, jnp.float32)
        for c in range(chunks):
            cols = slice(c * BK, (c + 1) * BK)
            s = dot_t(q, k_s[cols, :])
            if c == 0:
                s = s + mask_s[0:1, :]
            s_s[:, cols] = s
            for t in range(BK // 128):
                top = jnp.maximum(top, s[:, t * 128 : (t + 1) * 128])
        row_max = jnp.max(top, axis=1, keepdims=True)
        total = jnp.zeros((BQ, 128), jnp.float32)
        a = jnp.zeros((BQ, HEAD), jnp.float32)
        for c in range(chunks):
            cols = slice(c * BK, (c + 1) * BK)
            e = jnp.exp2((s_s[:, cols] - row_max) * SCALE2)
            for t in range(BK // 128):
                total = total + e[:, t * 128 : (t + 1) * 128]
            eb = e.astype(jnp.bfloat16)
            e_s[:, cols] = eb
            a = a + dot(eb, v_s[cols, :])
        inv = 1.0 / jnp.sum(total, axis=1, keepdims=True)
        ab = (a * inv).astype(jnp.bfloat16)
        gs = (g.astype(jnp.float32) * inv).astype(jnp.bfloat16)
        delta = jnp.sum(gs.astype(jnp.float32) * ab.astype(jnp.float32), axis=1, keepdims=True)
        gt = gs.T
        qt = q.T
        dq = jnp.zeros((BQ, HEAD), jnp.float32)
        for c in range(chunks):
            cols = slice(c * BK, (c + 1) * BK)
            eb = e_s[:, cols]
            dp = dot_t(gs, v_s[cols, :])
            ds = eb * (dp - delta).astype(jnp.bfloat16)
            dv_s[:, cols] += dot(gt, eb)
            dk_s[:, cols] += dot(qt, ds)
            dq = dq + dot(ds, k_s[cols, :])
        aq[0, rows, :] = ab
        aq[1, rows, :] = (dq * SCALE).astype(jnp.bfloat16)

    for i in range(NQ // BQ):
        block(i)
    for t, src, factor in ((0, dk_s, SCALE), (1, dv_s, 1.0)):
        for h, dst in ((0, part_own), (1, part_oth)):
            xt = src[:, h * half_txt : (h + 1) * half_txt].T * factor
            at = TXT_KEYS + h * half_img
            xi = src[:, at : at + half_img].T * factor
            for s in range(CHIPS):
                dst[s, t, :TXT, :] = xt[s * TXT : (s + 1) * TXT]
                dst[s, t, TXT:, :] = xi[s * IMG : (s + 1) * IMG]


def combine_kernel(aq, mine, theirs, out):
    for s in range(CHIPS):
        for t in range(2):
            out[s, t] = aq[t, s * ROWS : (s + 1) * ROWS, :]
            out[s, 2 + t] = (mine[s, t] + theirs[s, t]).astype(jnp.bfloat16)


def unpack_kernel(back, residual, gain, ta, io, tg, ig):
    for h in range(HEADS):
        cols = slice(h * HEAD, (h + 1) * HEAD)
        ta[:, cols] = back[h, 0, :TXT, :]
        io[:, cols] = (
            back[h, 0, TXT:, :].astype(jnp.float32)
            + gain[0:1, cols] * residual[:, cols].astype(jnp.float32)
        ).astype(jnp.bfloat16)
        for t in range(3):
            tg[t, :, cols] = back[h, 1 + t, :TXT, :]
            ig[t, :, cols] = back[h, 1 + t, TXT:, :]


def call(kernel, ins, outs, scratch=(), **kw):
    return pl.pallas_call(
        kernel,
        in_specs=ins,
        out_specs=[VM] * len(outs) if len(outs) > 1 else VM,
        out_shape=[jax.ShapeDtypeStruct(s, d) for s, d in outs]
        if len(outs) > 1
        else jax.ShapeDtypeStruct(*outs[0]),
        scratch_shapes=scratch,
        compiler_params=pltpu.CompilerParams(vmem_limit_bytes=48 << 20),
        **kw,
    )


def body(th, ih, tc, ic, residual, gain, lengths):
    bf16, f32 = jnp.bfloat16, jnp.float32
    chips = ("x", "yl")
    grp = ("yh", "z")
    width = HEADS * HEAD
    core = lax.axis_index("core")
    info = jnp.stack([lengths[0], core.astype(jnp.int32)])
    send = call(pack_kernel, [VM] * 4, [((HEADS, 4, ROWS, HEAD), bf16)], name="pack")(
        jnp.swapaxes(th[0], 0, 1), jnp.swapaxes(ih[0], 0, 1), tc[0], ic[0]
    )
    own = lax.all_to_all(send, chips, split_axis=0, concat_axis=0, tiled=True)
    swap = [(0, 1), (1, 0)]
    oth = lax.ppermute(own, "core", swap)
    outgoing = (gain[None, :] * ic[0].astype(f32)).astype(bf16).reshape(residual.shape)
    control = lax.all_to_all(
        jnp.stack([residual, outgoing], axis=1), grp, split_axis=0, concat_axis=0, tiled=True
    )
    part = ((CHIPS, 2, ROWS, HEAD), f32)
    aq, mine, give = call(
        attention_kernel,
        [SM, VM, VM],
        [((2, NQ, HEAD), bf16), part, part],
        [
            pltpu.VMEM((NQ, HEAD), bf16),
            pltpu.VMEM((NQ, HEAD), bf16),
            pltpu.VMEM((NK, HEAD), bf16),
            pltpu.VMEM((NK, HEAD), bf16),
            pltpu.VMEM((BQ, NK), f32),
            pltpu.VMEM((BQ, NK), bf16),
            pltpu.VMEM((HEAD, NK), f32),
            pltpu.VMEM((HEAD, NK), f32),
            pltpu.VMEM((8, TXT_KEYS), f32),
        ],
        name="attention",
        cost_estimate=pl.CostEstimate(
            flops=14 * NQ * NK * HEAD, bytes_accessed=8 << 20, transcendentals=NQ * NK
        ),
    )(info, own, oth)
    theirs = lax.ppermute(give, "core", swap)
    ready = call(combine_kernel, [VM] * 3, [((CHIPS, 4, ROWS, HEAD), bf16)], name="combine")(
        aq, mine, theirs
    )
    back = lax.all_to_all(ready, chips, split_axis=0, concat_axis=0, tiled=True)
    arrived = control[:, 0].reshape(IMG, width)
    ta, io, tg, ig = call(
        unpack_kernel,
        [VM] * 3,
        [((TXT, width), bf16), ((IMG, width), bf16), ((3, TXT, width), bf16), ((3, IMG, width), bf16)],
        name="unpack",
    )(back, arrived, gain[None, :])
    return (
        ta[None],
        io[None],
        jnp.swapaxes(tg, 0, 1)[None],
        jnp.swapaxes(ig, 0, 1)[None],
        control[:, 1],
    )


def solution(mesh):
    fine = Mesh(mesh.devices.reshape(2, 8, 4, 4, 2), ("yh", "z", "x", "yl", "core"))
    grp = ("yh", "z")
    seq = ("x", "yl", "core")
    in_specs = (
        P(grp, seq, None, None),
        P(grp, seq, None, None),
        P(grp, seq, None),
        P(grp, seq, None),
        P(None, seq, grp, None),
        P(),
        P(grp),
    )
    out_specs = (
        P(grp, seq, None),
        P(grp, seq, None),
        P(grp, seq, None, None),
        P(grp, seq, None, None),
        P(None, seq, grp, None),
    )
    return jax.shard_map(body, mesh=fine, in_specs=in_specs, out_specs=out_specs, check_vma=False)
```

```python
import functools
import math

import jax
import jax.numpy as jnp
from jax import lax
from jax.experimental import pallas as pl
from jax.experimental.pallas import tpu as pltpu
from jax.sharding import Mesh, PartitionSpec as P

HEAD = 128
HEADS = 16
TXT = 16
IMG = 64
ROWS = TXT + IMG
ZS = 8
EARLY = 5
CHIPS = 16
SCALE = 1.0 / math.sqrt(HEAD)
SCALE2 = SCALE * math.log2(math.e)
BQ = 256
BK = 512
NQ = CHIPS * ROWS
NK = 2 * NQ
TXT_KEYS = 2 * CHIPS * TXT

VM = pl.BlockSpec(memory_space=pltpu.VMEM)
SM = pl.BlockSpec(memory_space=pltpu.SMEM)
HBM = pl.BlockSpec(memory_space=pltpu.HBM)


def dot(a, b):
    return lax.dot_general(a, b, (((1,), (0,)), ((), ())), preferred_element_type=jnp.float32)


def dot_t(a, b):
    return lax.dot_general(a, b, (((1,), (1,)), ((), ())), preferred_element_type=jnp.float32)


def pack_kernel(th, ih, tc, ic, out, th_s, ih_s, tc_s, ic_s, sems):
    copies = []
    for t in range(3):
        copies.append((ih.at[t], ih_s.at[t]))
        copies.append((th.at[t], th_s.at[t]))
    copies += [(ic, ic_s), (tc, tc_s)]
    copies = [pltpu.make_async_copy(a, b, sems.at[n]) for n, (a, b) in enumerate(copies)]
    for c in copies:
        c.start()
    for c in copies:
        c.wait()
    for h in range(HEADS):
        cols = slice(h * HEAD, (h + 1) * HEAD)
        for t in range(3):
            out[h, t, :TXT, :] = th_s[t, :, cols]
            out[h, t, TXT:, :] = ih_s[t, :, cols]
        out[h, 3, :TXT, :] = tc_s[:, cols]
        out[h, 3, TXT:, :] = ic_s[:, cols]


def control_pack_kernel(info, residual, ic, gain, *refs):
    outs, scaled = refs[:ZS], refs[ZS]
    yh, z = info[2], info[3]
    for r in range(IMG // 16):
        x = ic[r * 16 : (r + 1) * 16, :].astype(jnp.float32) * gain[0:1, :]
        for i in range(4):
            scaled[r * 4 + i] = x[i * 4 : (i + 1) * 4].astype(jnp.bfloat16)
    for k in range(ZS):
        for rel in range(2):
            g = (yh if rel == 0 else 1 - yh) * ZS + lax.rem(z + k, ZS)
            outs[k][rel, 0] = residual[g]
            outs[k][rel, 1] = scaled[g]


def control_unpack_kernel(info, *refs):
    near, far, late = refs[:EARLY], refs[EARLY], refs[EARLY + 1 : ZS + 1]
    grads, arrived, rows = refs[ZS + 1 :]
    yh, z = info[2], info[3]
    for k in range(ZS):
        for rel in range(2):
            g = (yh if rel == 0 else 1 - yh) * ZS + lax.rem(z + ZS - k, ZS)
            if k >= EARLY:
                src = late[k - EARLY].at[rel]
            else:
                src = near[k].at[0] if rel == 0 else far.at[k]
            rows[g] = src[0]
            grads[g] = src[1]
    for r in range(IMG // 16):
        part = [rows[r * 4 + i].astype(jnp.float32) for i in range(4)]
        arrived[r * 16 : (r + 1) * 16, :] = jnp.concatenate(part, axis=0).astype(jnp.bfloat16)


def attention_kernel(
    info, own, oth, aq, part_own, part_oth, q_s, g_s, k_s, v_s, s_s, e_s, dk_s, dv_s, mask_s
):
    length = info[0]
    core = info[1]
    half_txt = CHIPS * TXT
    half_img = CHIPS * IMG
    for s in range(CHIPS):
        q_s[s * ROWS : (s + 1) * ROWS, :] = own[s, 0]
        g_s[s * ROWS : (s + 1) * ROWS, :] = own[s, 3]
        for h, src in ((0, own), (1, oth)):
            for t, dst in ((1, k_s), (2, v_s)):
                at = h * half_txt + s * TXT
                dst[at : at + TXT, :] = src[s, t, :TXT, :]
                at = TXT_KEYS + h * half_img + s * IMG
                dst[at : at + IMG, :] = src[s, t, TXT:, :]
    pos = lax.broadcasted_iota(jnp.int32, (8, TXT_KEYS), 1)
    half = jnp.where(pos < half_txt, core, 1 - core)
    token = ((pos % half_txt) // TXT) * (2 * TXT) + half * TXT + pos % TXT
    mask_s[...] = jnp.where(token < length, 0.0, -jnp.inf)
    dk_s[...] = jnp.zeros_like(dk_s)
    dv_s[...] = jnp.zeros_like(dv_s)
    chunks = NK // BK

    def block(i):
        rows = slice(i * BQ, (i + 1) * BQ)
        q = q_s[rows, :]
        g = g_s[rows, :]
        top = jnp.full((BQ, 128), -jnp.inf, jnp.float32)
        for c in range(chunks):
            cols = slice(c * BK, (c + 1) * BK)
            s = dot_t(q, k_s[cols, :])
            if c == 0:
                s = s + mask_s[0:1, :]
            s_s[:, cols] = s
            for t in range(BK // 128):
                top = jnp.maximum(top, s[:, t * 128 : (t + 1) * 128])
        row_max = jnp.max(top, axis=1, keepdims=True)
        total = jnp.zeros((BQ, 128), jnp.float32)
        a = jnp.zeros((BQ, HEAD), jnp.float32)
        for c in range(chunks):
            cols = slice(c * BK, (c + 1) * BK)
            e = jnp.exp2((s_s[:, cols] - row_max) * SCALE2)
            for t in range(BK // 128):
                total = total + e[:, t * 128 : (t + 1) * 128]
            eb = e.astype(jnp.bfloat16)
            e_s[:, cols] = eb
            a = a + dot(eb, v_s[cols, :])
        inv = 1.0 / jnp.sum(total, axis=1, keepdims=True)
        ab = (a * inv).astype(jnp.bfloat16)
        gs = (g.astype(jnp.float32) * inv).astype(jnp.bfloat16)
        delta = jnp.sum(gs.astype(jnp.float32) * ab.astype(jnp.float32), axis=1, keepdims=True)
        gt = gs.T
        qt = q.T
        dq = jnp.zeros((BQ, HEAD), jnp.float32)
        for c in range(chunks):
            cols = slice(c * BK, (c + 1) * BK)
            eb = e_s[:, cols]
            dp = dot_t(gs, v_s[cols, :])
            ds = eb * (dp - delta).astype(jnp.bfloat16)
            dv_s[:, cols] += dot(gt, eb)
            dk_s[:, cols] += dot(qt, ds)
            dq = dq + dot(ds, k_s[cols, :])
        aq[0, rows, :] = ab
        aq[1, rows, :] = (dq * SCALE).astype(jnp.bfloat16)

    for i in range(NQ // BQ):
        block(i)
    for t, src, factor in ((0, dk_s, SCALE), (1, dv_s, 1.0)):
        for h, dst in ((0, part_own), (1, part_oth)):
            xt = src[:, h * half_txt : (h + 1) * half_txt].T * factor
            at = TXT_KEYS + h * half_img
            xi = src[:, at : at + half_img].T * factor
            for s in range(CHIPS):
                dst[s, t, :TXT, :] = xt[s * TXT : (s + 1) * TXT]
                dst[s, t, TXT:, :] = xi[s * IMG : (s + 1) * IMG]


def combine_kernel(aq, mine, theirs, out):
    for s in range(CHIPS):
        for t in range(2):
            out[s, t] = aq[t, s * ROWS : (s + 1) * ROWS, :]
            out[s, 2 + t] = (mine[s, t] + theirs[s, t]).astype(jnp.bfloat16)


def unpack_kernel(back, residual, gain, ta, io, tg, ig):
    for h in range(HEADS):
        cols = slice(h * HEAD, (h + 1) * HEAD)
        ta[:, cols] = back[h, 0, :TXT, :]
        io[:, cols] = (
            back[h, 0, TXT:, :].astype(jnp.float32)
            + gain[0:1, cols] * residual[:, cols].astype(jnp.float32)
        ).astype(jnp.bfloat16)
        for t in range(3):
            tg[t, :, cols] = back[h, 1 + t, :TXT, :]
            ig[t, :, cols] = back[h, 1 + t, TXT:, :]


def call(kernel, ins, outs, scratch=(), vmem=8, **kw):
    return pl.pallas_call(
        kernel,
        in_specs=ins,
        out_specs=[VM] * len(outs) if len(outs) > 1 else VM,
        out_shape=[jax.ShapeDtypeStruct(s, d) for s, d in outs]
        if len(outs) > 1
        else jax.ShapeDtypeStruct(*outs[0]),
        scratch_shapes=scratch,
        compiler_params=pltpu.CompilerParams(vmem_limit_bytes=vmem << 20),
        **kw,
    )


def body(th, ih, tc, ic, residual, gain, lengths):
    bf16, f32 = jnp.bfloat16, jnp.float32
    chips = ("x", "yl")
    grp = ("yh", "z")
    width = HEADS * HEAD
    core = lax.axis_index("core")
    index = [core, lax.axis_index("yh"), lax.axis_index("z")]
    info = jnp.stack([lengths[0]] + [i.astype(jnp.int32) for i in index])
    send = call(
        pack_kernel,
        [HBM] * 4,
        [((HEADS, 4, ROWS, HEAD), bf16)],
        [
            pltpu.VMEM((3, TXT, width), bf16),
            pltpu.VMEM((3, IMG, width), bf16),
            pltpu.VMEM((TXT, width), bf16),
            pltpu.VMEM((IMG, width), bf16),
            pltpu.SemaphoreType.DMA((8,)),
        ],
        vmem=63,
        name="pack",
    )(jnp.swapaxes(th[0], 0, 1), jnp.swapaxes(ih[0], 0, 1), tc[0], ic[0])
    send, late_ic = lax.optimization_barrier((send, ic[0]))
    own = lax.all_to_all(send, chips, split_axis=0, concat_axis=0, tiled=True)
    swap = [(0, 1), (1, 0)]
    piece = (2, 2, 4, width)
    pieces = call(
        control_pack_kernel,
        [SM] + [VM] * 3,
        [(piece, bf16)] * ZS,
        [pltpu.VMEM((16, 4, width), bf16)],
        name="control_pack",
    )(info, residual[:, 0], late_ic, gain[None, :])

    def shift(x, k):
        return lax.ppermute(x, "z", [(i, (i + k) % ZS) for i in range(ZS)])

    pieces = list(pieces)
    near = pieces[:1] + [shift(pieces[k], k) for k in range(1, EARLY)]
    own, *near = lax.optimization_barrier([own] + near)
    oth = lax.ppermute(own, "core", swap)
    far = lax.ppermute(jnp.stack([p[1] for p in near + pieces[EARLY:]]), "yh", swap)
    part = ((CHIPS, 2, ROWS, HEAD), f32)
    aq, mine, give = call(
        attention_kernel,
        [SM, VM, VM],
        [((2, NQ, HEAD), bf16), part, part],
        [
            pltpu.VMEM((NQ, HEAD), bf16),
            pltpu.VMEM((NQ, HEAD), bf16),
            pltpu.VMEM((NK, HEAD), bf16),
            pltpu.VMEM((NK, HEAD), bf16),
            pltpu.VMEM((BQ, NK), f32),
            pltpu.VMEM((BQ, NK), bf16),
            pltpu.VMEM((HEAD, NK), f32),
            pltpu.VMEM((HEAD, NK), f32),
            pltpu.VMEM((8, TXT_KEYS), f32),
        ],
        vmem=20,
        name="attention",
        cost_estimate=pl.CostEstimate(
            flops=14 * NQ * NK * HEAD, bytes_accessed=8 << 20, transcendentals=NQ * NK
        ),
    )(info, own, oth)
    give, far = lax.optimization_barrier((give, far))
    theirs = lax.ppermute(give, "core", swap)
    ready = call(combine_kernel, [VM] * 3, [((CHIPS, 4, ROWS, HEAD), bf16)], name="combine")(
        aq, mine, theirs
    )
    late = [jnp.stack([pieces[k][0], far[k]]) for k in range(EARLY, ZS)]
    ready, *late = lax.optimization_barrier([ready] + late)
    late = [shift(x, EARLY + n) for n, x in enumerate(late)]
    back = lax.all_to_all(ready, chips, split_axis=0, concat_axis=0, tiled=True)
    grads, arrived = call(
        control_unpack_kernel,
        [SM] + [VM] * (ZS + 1),
        [((16, 4, width), bf16), ((IMG, width), bf16)],
        [pltpu.VMEM((16, 4, width), bf16)],
        name="control_unpack",
    )(info, *near, far, *late)
    ta, io, tg, ig = call(
        unpack_kernel,
        [VM] * 3,
        [((TXT, width), bf16), ((IMG, width), bf16), ((3, TXT, width), bf16), ((3, IMG, width), bf16)],
        name="unpack",
    )(back, arrived, gain[None, :])
    return (
        ta[None],
        io[None],
        jnp.swapaxes(tg, 0, 1)[None],
        jnp.swapaxes(ig, 0, 1)[None],
        grads[:, None],
    )


def solution(mesh):
    fine = Mesh(mesh.devices.reshape(2, 8, 4, 4, 2), ("yh", "z", "x", "yl", "core"))
    grp = ("yh", "z")
    seq = ("x", "yl", "core")
    in_specs = (
        P(grp, seq, None, None),
        P(grp, seq, None, None),
        P(grp, seq, None),
        P(grp, seq, None),
        P(None, seq, grp, None),
        P(),
        P(grp),
    )
    out_specs = (
        P(grp, seq, None),
        P(grp, seq, None),
        P(grp, seq, None, None),
        P(grp, seq, None, None),
        P(None, seq, grp, None),
    )
    return jax.shard_map(body, mesh=fine, in_specs=in_specs, out_specs=out_specs, check_vma=False)
```

```python
import functools
import math

import jax
import jax.numpy as jnp
from jax import lax
from jax.experimental import pallas as pl
from jax.experimental.pallas import tpu as pltpu
from jax.sharding import Mesh, PartitionSpec as P

HEAD = 128
HEADS = 16
TXT = 16
IMG = 64
ROWS = TXT + IMG
ZS = 8
EARLY = 5
CHIPS = 16
SCALE = 1.0 / math.sqrt(HEAD)
SCALE2 = SCALE * math.log2(math.e)
BQ = 256
NQ = CHIPS * ROWS
NK = 2 * NQ
HALF_TXT = CHIPS * TXT

VM = pl.BlockSpec(memory_space=pltpu.VMEM)
SM = pl.BlockSpec(memory_space=pltpu.SMEM)
ANY = pl.BlockSpec(memory_space=pl.ANY)
HBM = pl.BlockSpec(memory_space=pltpu.HBM)


def dot(a, b):
    return lax.dot_general(a, b, (((1,), (0,)), ((), ())), preferred_element_type=jnp.float32)


def dot_t(a, b):
    return lax.dot_general(a, b, (((1,), (1,)), ((), ())), preferred_element_type=jnp.float32)


def pack_kernel(th, ih, tc, ic, out, th_s, ih_s, tc_s, ic_s, out_s, in_sems, out_sems):
    pairs = [(ih.at[t], ih_s.at[t], th.at[t], th_s.at[t]) for t in range(3)]
    pairs.append((ic, ic_s, tc, tc_s))
    copies = []
    for n, (a, b, c, d) in enumerate(pairs):
        copies.append(
            (
                pltpu.make_async_copy(a, b, in_sems.at[n, 0]),
                pltpu.make_async_copy(c, d, in_sems.at[n, 1]),
            )
        )
    for image, text in copies:
        image.start()
        text.start()
    leaving = []
    for t, (image, text) in enumerate(copies):
        image.wait()
        text.wait()
        for h in range(HEADS):
            cols = slice(h * HEAD, (h + 1) * HEAD)
            out_s[t, h, :TXT, :] = th_s[t, :, cols] if t < 3 else tc_s[:, cols]
            out_s[t, h, TXT:, :] = ih_s[t, :, cols] if t < 3 else ic_s[:, cols]
        leaving.append(pltpu.make_async_copy(out_s.at[t], out.at[:, t], out_sems.at[t]))
        leaving[-1].start()
    for copy in leaving:
        copy.wait()


def control_pack_kernel(info, residual, ic, gain, *refs):
    outs, scaled = refs[:ZS], refs[ZS]
    yh, z = info[2], info[3]
    for r in range(IMG // 16):
        x = ic[r * 16 : (r + 1) * 16, :].astype(jnp.float32) * gain[0:1, :]
        for i in range(4):
            scaled[r * 4 + i] = x[i * 4 : (i + 1) * 4].astype(jnp.bfloat16)
    for k in range(ZS):
        for rel in range(2):
            g = (yh if rel == 0 else 1 - yh) * ZS + lax.rem(z + k, ZS)
            outs[k][rel, 0] = residual[g]
            outs[k][rel, 1] = scaled[g]


def control_unpack_kernel(info, *refs):
    near, far, late = refs[:EARLY], refs[EARLY], refs[EARLY + 1 : ZS + 1]
    grads, arrived, rows = refs[ZS + 1 :]
    yh, z = info[2], info[3]
    for k in range(ZS):
        for rel in range(2):
            g = (yh if rel == 0 else 1 - yh) * ZS + lax.rem(z + ZS - k, ZS)
            if k >= EARLY:
                src = late[k - EARLY].at[rel]
            else:
                src = near[k].at[0] if rel == 0 else far.at[k]
            rows[g] = src[0]
            grads[g] = src[1]
    for r in range(IMG // 16):
        part = [rows[r * 4 + i].astype(jnp.float32) for i in range(4)]
        arrived[r * 16 : (r + 1) * 16, :] = jnp.concatenate(part, axis=0).astype(jnp.bfloat16)


def attention_kernel(
    info, own, oth, part, give, e_own, ds_own, qgt, q_s, g_s, k_s, v_s, s_s, e_oth, ds_oth, mask_s
):
    length = info[0]
    core = info[1]
    for s in range(CHIPS):
        q_s[s * ROWS : (s + 1) * ROWS, :] = own[s, 0]
        g_s[s * ROWS : (s + 1) * ROWS, :] = own[s, 3]
        for h, src in ((0, own), (1, oth)):
            for t, dst in ((1, k_s), (2, v_s)):
                at = h * NQ + s * TXT
                dst[at : at + TXT, :] = src[s, t, :TXT, :]
                at = h * NQ + HALF_TXT + s * IMG
                dst[at : at + IMG, :] = src[s, t, TXT:, :]
    pos = lax.broadcasted_iota(jnp.int32, (8, HALF_TXT), 1)
    for h in range(2):
        first = (core if h == 0 else 1 - core) * TXT
        token = (pos // TXT) * (2 * TXT) + first + pos % TXT
        mask_s[h] = jnp.where(token < length, 0.0, -jnp.inf)

    def place(i, t, x):
        at, end = i * BQ, (i + 1) * BQ
        while at < end:
            s, r = divmod(at, ROWS)
            n = min(ROWS - r, end - at)
            part[s, t, r : r + n, :] = x[at - i * BQ : at - i * BQ + n]
            at += n

    def block(i):
        rows = slice(i * BQ, (i + 1) * BQ)
        q = q_s[rows, :]
        g = g_s[rows, :]
        top = None
        for h in range(2):
            s = dot_t(q, k_s[h * NQ : (h + 1) * NQ, :])
            text = s[:, :HALF_TXT] + mask_s[h, 0:1, :]
            s_s[:, h * NQ : h * NQ + HALF_TXT] = text
            s_s[:, h * NQ + HALF_TXT : (h + 1) * NQ] = s[:, HALF_TXT:]
            for t in range(NQ // 128):
                x = (text if t < HALF_TXT // 128 else s)[:, t * 128 : (t + 1) * 128]
                top = x if top is None else jnp.maximum(top, x)
        row_max = jnp.max(top, axis=1, keepdims=True)
        a = total = None
        for h, dst in ((0, e_own), (1, e_oth)):
            cols = slice(h * NQ, (h + 1) * NQ)
            e = jnp.exp2((s_s[:, cols] - row_max) * SCALE2)
            for t in range(NQ // 128):
                x = e[:, t * 128 : (t + 1) * 128]
                total = x if total is None else total + x
            e = e.astype(jnp.bfloat16)
            dst[rows, :] = e
            x = dot(e, v_s[cols, :])
            a = x if a is None else a + x
        inv = 1.0 / jnp.sum(total, axis=1, keepdims=True)
        ab = (a * inv).astype(jnp.bfloat16)
        gs = (g.astype(jnp.float32) * inv).astype(jnp.bfloat16)
        delta = jnp.sum(gs.astype(jnp.float32) * ab.astype(jnp.float32), axis=1, keepdims=True)
        place(i, 0, ab)
        qgt[0, :, rows] = q.T
        qgt[1, :, rows] = gs.T
        dq = None
        for h, src, dst in ((0, e_own, ds_own), (1, e_oth, ds_oth)):
            cols = slice(h * NQ, (h + 1) * NQ)
            dp = dot_t(gs, v_s[cols, :]) - delta
            ds = src[rows, :] * dp.astype(jnp.bfloat16)
            dst[rows, :] = ds
            x = dot(ds, k_s[cols, :])
            dq = x if dq is None else dq + x
        place(i, 1, (dq * SCALE).astype(jnp.bfloat16))

    for i in range(NQ // BQ):
        block(i)
    give[0] = (dot(qgt[0], ds_oth[...]) * SCALE).astype(jnp.bfloat16)
    give[1] = dot(qgt[1], e_oth[...]).astype(jnp.bfloat16)


def key_grad_kernel(qgt, e_own, ds_own, mine):
    mine[0] = dot(qgt[0], ds_own[...]) * SCALE
    mine[1] = dot(qgt[1], e_own[...])


def combine_kernel(part, mine, theirs, out, x_s, sems):
    del part
    copies = []
    for t in range(2):
        x = (mine[t] + theirs[t].astype(jnp.float32)).astype(jnp.bfloat16).T
        for s in range(CHIPS):
            x_s[t, s, :TXT, :] = x[s * TXT : (s + 1) * TXT]
            x_s[t, s, TXT:, :] = x[HALF_TXT + s * IMG : HALF_TXT + (s + 1) * IMG]
        copies.append(pltpu.make_async_copy(x_s.at[t], out.at[:, 2 + t], sems.at[t]))
        copies[-1].start()
    for copy in copies:
        copy.wait()


def unpack_kernel(back, residual, gain, ta, io, tg, ig, ta_s, io_s, tg_s, ig_s, sems):
    copies = []

    def send(a, b):
        copies.append(pltpu.make_async_copy(a, b, sems.at[len(copies)]))
        copies[-1].start()

    for t in range(3):
        for h in range(HEADS):
            cols = slice(h * HEAD, (h + 1) * HEAD)
            tg_s[t, :, cols] = back[h, 1 + t, :TXT, :]
            ig_s[t, :, cols] = back[h, 1 + t, TXT:, :]
        send(ig_s.at[t], ig.at[t])
        send(tg_s.at[t], tg.at[t])
    for h in range(HEADS):
        cols = slice(h * HEAD, (h + 1) * HEAD)
        ta_s[:, cols] = back[h, 0, :TXT, :]
        io_s[:, cols] = (
            back[h, 0, TXT:, :].astype(jnp.float32)
            + gain[0:1, cols] * residual[:, cols].astype(jnp.float32)
        ).astype(jnp.bfloat16)
    send(io_s, io)
    send(ta_s, ta)
    for copy in copies:
        copy.wait()


def call(kernel, ins, outs, scratch=(), vmem=8, out_place=VM, **kw):
    return pl.pallas_call(
        kernel,
        in_specs=ins,
        out_specs=[out_place] * len(outs) if len(outs) > 1 else out_place,
        out_shape=[jax.ShapeDtypeStruct(s, d) for s, d in outs]
        if len(outs) > 1
        else jax.ShapeDtypeStruct(*outs[0]),
        scratch_shapes=scratch,
        compiler_params=pltpu.CompilerParams(vmem_limit_bytes=vmem << 20),
        **kw,
    )


def body(th, ih, tc, ic, residual, gain, lengths):
    bf16, f32 = jnp.bfloat16, jnp.float32
    chips = ("x", "yl")
    grp = ("yh", "z")
    width = HEADS * HEAD
    core = lax.axis_index("core")
    index = [core, lax.axis_index("yh"), lax.axis_index("z")]
    info = jnp.stack([lengths[0]] + [i.astype(jnp.int32) for i in index])
    send = call(
        pack_kernel,
        [HBM] * 4,
        [((HEADS, 4, ROWS, HEAD), bf16)],
        out_place=HBM,
        scratch=[
            pltpu.VMEM((3, TXT, width), bf16),
            pltpu.VMEM((3, IMG, width), bf16),
            pltpu.VMEM((TXT, width), bf16),
            pltpu.VMEM((IMG, width), bf16),
            pltpu.VMEM((4, HEADS, ROWS, HEAD), bf16),
            pltpu.SemaphoreType.DMA((4, 2)),
            pltpu.SemaphoreType.DMA((4,)),
        ],
        vmem=63,
        name="pack",
    )(jnp.swapaxes(th[0], 0, 1), jnp.swapaxes(ih[0], 0, 1), tc[0], ic[0])
    send, late_ic = lax.optimization_barrier((send, ic[0]))
    own = lax.all_to_all(send, chips, split_axis=0, concat_axis=0, tiled=True)
    swap = [(0, 1), (1, 0)]
    piece = (2, 2, 4, width)
    pieces = call(
        control_pack_kernel,
        [SM] + [VM] * 3,
        [(piece, bf16)] * ZS,
        [pltpu.VMEM((16, 4, width), bf16)],
        name="control_pack",
    )(info, residual[:, 0], late_ic, gain[None, :])

    def shift(x, k):
        return lax.ppermute(x, "z", [(i, (i + k) % ZS) for i in range(ZS)])

    pieces = list(pieces)
    near = pieces[:1] + [shift(pieces[k], k) for k in range(1, EARLY)]
    own, *near = lax.optimization_barrier([own] + near)
    oth = lax.ppermute(own, "core", swap)
    far = lax.ppermute(jnp.stack([p[1] for p in near + pieces[EARLY:]]), "yh", swap)
    square = ((NQ, NQ), bf16)
    turned = ((2, HEAD, NQ), bf16)
    part, give, e_own, ds_own, qgt = call(
        attention_kernel,
        [SM, VM, VM],
        [((CHIPS, 4, ROWS, HEAD), bf16), turned, square, square, turned],
        [
            pltpu.VMEM((NQ, HEAD), bf16),
            pltpu.VMEM((NQ, HEAD), bf16),
            pltpu.VMEM((NK, HEAD), bf16),
            pltpu.VMEM((NK, HEAD), bf16),
            pltpu.VMEM((BQ, NK), f32),
            pltpu.VMEM((NQ, NQ), bf16),
            pltpu.VMEM((NQ, NQ), bf16),
            pltpu.VMEM((2, 8, HALF_TXT), f32),
        ],
        vmem=32,
        name="attention",
        cost_estimate=pl.CostEstimate(
            flops=12 * NQ * NK * HEAD, bytes_accessed=8 << 20, transcendentals=NQ * NK
        ),
    )(info, own, oth)
    theirs = lax.ppermute(give, "core", swap)
    qgt, far = lax.optimization_barrier((qgt, far))
    mine = call(key_grad_kernel, [VM] * 3, [((2, HEAD, NQ), f32)], vmem=16, name="key_grad")(
        qgt, e_own, ds_own
    )
    ready = call(
        combine_kernel,
        [ANY, VM, VM],
        [((CHIPS, 4, ROWS, HEAD), bf16)],
        out_place=ANY,
        scratch=[pltpu.VMEM((2, CHIPS, ROWS, HEAD), bf16), pltpu.SemaphoreType.DMA((2,))],
        input_output_aliases={0: 0},
        name="combine",
    )(part, mine, theirs)
    late = [jnp.stack([pieces[k][0], far[k]]) for k in range(EARLY, ZS)]
    ready, *late = lax.optimization_barrier([ready] + late)
    late = [shift(x, EARLY + n) for n, x in enumerate(late)]
    back = lax.all_to_all(ready, chips, split_axis=0, concat_axis=0, tiled=True)
    grads, arrived = call(
        control_unpack_kernel,
        [SM] + [VM] * (ZS + 1),
        [((16, 4, width), bf16), ((IMG, width), bf16)],
        [pltpu.VMEM((16, 4, width), bf16)],
        name="control_unpack",
    )(info, *near, far, *late)
    results = [((TXT, width), bf16), ((IMG, width), bf16)]
    results += [((3, TXT, width), bf16), ((3, IMG, width), bf16)]
    ta, io, tg, ig = call(
        unpack_kernel,
        [VM] * 3,
        results,
        out_place=HBM,
        scratch=[pltpu.VMEM(*r) for r in results] + [pltpu.SemaphoreType.DMA((8,))],
        name="unpack",
    )(back, arrived, gain[None, :])
    return (
        ta[None],
        io[None],
        jnp.swapaxes(tg, 0, 1)[None],
        jnp.swapaxes(ig, 0, 1)[None],
        grads[:, None],
    )


def solution(mesh):
    fine = Mesh(mesh.devices.reshape(2, 8, 4, 4, 2), ("yh", "z", "x", "yl", "core"))
    grp = ("yh", "z")
    seq = ("x", "yl", "core")
    in_specs = (
        P(grp, seq, None, None),
        P(grp, seq, None, None),
        P(grp, seq, None),
        P(grp, seq, None),
        P(None, seq, grp, None),
        P(),
        P(grp),
    )
    out_specs = (
        P(grp, seq, None),
        P(grp, seq, None),
        P(grp, seq, None, None),
        P(grp, seq, None, None),
        P(None, seq, grp, None),
    )
    return jax.shard_map(body, mesh=fine, in_specs=in_specs, out_specs=out_specs, check_vma=False)
```

```python
import functools
import math

import jax
import jax.numpy as jnp
from jax import lax
from jax.experimental import pallas as pl
from jax.experimental.pallas import tpu as pltpu
from jax.sharding import Mesh, PartitionSpec as P

HEAD = 128
HEADS = 16
TXT = 16
IMG = 64
ROWS = TXT + IMG
ZS = 8
EARLY = 5
CHIPS = 16
SCALE = 1.0 / math.sqrt(HEAD)
SCALE2 = SCALE * math.log2(math.e)
BQ = 256
NQ = CHIPS * ROWS
NK = 2 * NQ
HALF_TXT = CHIPS * TXT

VM = pl.BlockSpec(memory_space=pltpu.VMEM)
SM = pl.BlockSpec(memory_space=pltpu.SMEM)
ANY = pl.BlockSpec(memory_space=pl.ANY)
HBM = pl.BlockSpec(memory_space=pltpu.HBM)


def dot(a, b):
    return lax.dot_general(a, b, (((1,), (0,)), ((), ())), preferred_element_type=jnp.float32)


def dot_t(a, b):
    return lax.dot_general(a, b, (((1,), (1,)), ((), ())), preferred_element_type=jnp.float32)


def pack_kernel(th, ih, tc, ic, out, th_s, ih_s, tc_s, ic_s, out_s, in_sems, out_sems):
    pairs = [(ih.at[t], ih_s.at[t], th.at[t], th_s.at[t]) for t in range(3)]
    pairs.append((ic, ic_s, tc, tc_s))
    copies = []
    for n, (a, b, c, d) in enumerate(pairs):
        copies.append(
            (
                pltpu.make_async_copy(a, b, in_sems.at[n, 0]),
                pltpu.make_async_copy(c, d, in_sems.at[n, 1]),
            )
        )
    for image, text in copies:
        image.start()
        text.start()
    leaving = []
    for t, (image, text) in enumerate(copies):
        image.wait()
        text.wait()
        for h in range(HEADS):
            cols = slice(h * HEAD, (h + 1) * HEAD)
            out_s[t, h, :TXT, :] = th_s[t, :, cols] if t < 3 else tc_s[:, cols]
            out_s[t, h, TXT:, :] = ih_s[t, :, cols] if t < 3 else ic_s[:, cols]
        leaving.append(pltpu.make_async_copy(out_s.at[t], out.at[:, t], out_sems.at[t]))
        leaving[-1].start()
    for copy in leaving:
        copy.wait()


def control_pack_kernel(info, residual, ic, gain, *refs):
    outs, scaled = refs[:ZS], refs[ZS]
    yh, z = info[2], info[3]
    for r in range(IMG // 16):
        x = ic[r * 16 : (r + 1) * 16, :].astype(jnp.float32) * gain[0:1, :]
        for i in range(4):
            scaled[r * 4 + i] = x[i * 4 : (i + 1) * 4].astype(jnp.bfloat16)
    for k in range(ZS):
        for rel in range(2):
            g = (yh if rel == 0 else 1 - yh) * ZS + lax.rem(z + k, ZS)
            outs[k][rel, 0] = residual[g]
            outs[k][rel, 1] = scaled[g]


def control_unpack_kernel(info, *refs):
    near, far, late = refs[:EARLY], refs[EARLY], refs[EARLY + 1 : ZS + 1]
    grads, arrived, rows = refs[ZS + 1 :]
    yh, z = info[2], info[3]
    for k in range(ZS):
        for rel in range(2):
            g = (yh if rel == 0 else 1 - yh) * ZS + lax.rem(z + ZS - k, ZS)
            if k >= EARLY:
                src = late[k - EARLY].at[rel]
            else:
                src = near[k].at[0] if rel == 0 else far.at[k]
            rows[g] = src[0]
            grads[g] = src[1]
    for r in range(IMG // 16):
        part = [rows[r * 4 + i].astype(jnp.float32) for i in range(4)]
        arrived[r * 16 : (r + 1) * 16, :] = jnp.concatenate(part, axis=0).astype(jnp.bfloat16)


def attention_kernel(
    info, own, oth, part, give, e_own, ds_own, qgt, q_s, g_s, k_s, v_s, s_s, e_oth, ds_oth, mask_s
):
    length = info[0]
    core = info[1]
    for s in range(CHIPS):
        q_s[s * ROWS : (s + 1) * ROWS, :] = own[s, 0]
        g_s[s * ROWS : (s + 1) * ROWS, :] = own[s, 3]
        for h, src in ((0, own), (1, oth)):
            for t, dst in ((1, k_s), (2, v_s)):
                at = h * NQ + s * TXT
                dst[at : at + TXT, :] = src[s, t, :TXT, :]
                at = h * NQ + HALF_TXT + s * IMG
                dst[at : at + IMG, :] = src[s, t, TXT:, :]
    pos = lax.broadcasted_iota(jnp.int32, (8, HALF_TXT), 1)
    for h in range(2):
        first = (core if h == 0 else 1 - core) * TXT
        token = (pos // TXT) * (2 * TXT) + first + pos % TXT
        mask_s[h] = jnp.where(token < length, 0.0, -jnp.inf)

    def place(i, t, x):
        at, end = i * BQ, (i + 1) * BQ
        while at < end:
            s, r = divmod(at, ROWS)
            n = min(ROWS - r, end - at)
            part[s, t, r : r + n, :] = x[at - i * BQ : at - i * BQ + n]
            at += n

    def block(i):
        rows = slice(i * BQ, (i + 1) * BQ)
        q = q_s[rows, :]
        g = g_s[rows, :]
        top = None
        for h in range(2):
            s = dot_t(q, k_s[h * NQ : (h + 1) * NQ, :])
            text = s[:, :HALF_TXT] + mask_s[h, 0:1, :]
            s_s[:, h * NQ : h * NQ + HALF_TXT] = text
            s_s[:, h * NQ + HALF_TXT : (h + 1) * NQ] = s[:, HALF_TXT:]
            for t in range(NQ // 128):
                x = (text if t < HALF_TXT // 128 else s)[:, t * 128 : (t + 1) * 128]
                top = x if top is None else jnp.maximum(top, x)
        row_max = jnp.max(top, axis=1, keepdims=True)
        a = total = None
        for h, dst in ((0, e_own), (1, e_oth)):
            cols = slice(h * NQ, (h + 1) * NQ)
            e = jnp.exp2((s_s[:, cols] - row_max) * SCALE2)
            for t in range(NQ // 128):
                x = e[:, t * 128 : (t + 1) * 128]
                total = x if total is None else total + x
            e = e.astype(jnp.bfloat16)
            dst[rows, :] = e
            x = dot(e, v_s[cols, :])
            a = x if a is None else a + x
        inv = 1.0 / jnp.sum(total, axis=1, keepdims=True)
        ab = (a * inv).astype(jnp.bfloat16)
        gs = (g.astype(jnp.float32) * inv).astype(jnp.bfloat16)
        delta = jnp.sum(gs.astype(jnp.float32) * ab.astype(jnp.float32), axis=1, keepdims=True)
        place(i, 0, ab)
        qgt[0, :, rows] = q.T
        qgt[1, :, rows] = gs.T
        dq = None
        for h, src, dst in ((0, e_own, ds_own), (1, e_oth, ds_oth)):
            cols = slice(h * NQ, (h + 1) * NQ)
            dp = dot_t(gs, v_s[cols, :]) - delta
            ds = src[rows, :] * dp.astype(jnp.bfloat16)
            dst[rows, :] = ds
            x = dot(ds, k_s[cols, :])
            dq = x if dq is None else dq + x
        place(i, 1, (dq * SCALE).astype(jnp.bfloat16))

    for i in range(NQ // BQ):
        block(i)
    give[0] = (dot(qgt[0], ds_oth[...]) * SCALE).astype(jnp.bfloat16)
    give[1] = dot(qgt[1], e_oth[...]).astype(jnp.bfloat16)


def key_grad_kernel(qgt, e_own, ds_own, mine):
    mine[0] = dot(qgt[0], ds_own[...]) * SCALE
    mine[1] = dot(qgt[1], e_own[...])


def combine_kernel(part, mine, theirs, out, x_s, sems):
    del part
    copies = []
    for t in range(2):
        x = (mine[t] + theirs[t].astype(jnp.float32)).astype(jnp.bfloat16).T
        for s in range(CHIPS):
            x_s[t, s, :TXT, :] = x[s * TXT : (s + 1) * TXT]
            x_s[t, s, TXT:, :] = x[HALF_TXT + s * IMG : HALF_TXT + (s + 1) * IMG]
        copies.append(pltpu.make_async_copy(x_s.at[t], out.at[:, 2 + t], sems.at[t]))
        copies[-1].start()
    for copy in copies:
        copy.wait()


def unpack_kernel(back, residual, gain, ta, io, tg, ig, ta_s, io_s, tg_s, ig_s, sems):
    copies = []

    def send(a, b):
        copies.append(pltpu.make_async_copy(a, b, sems.at[len(copies)]))
        copies[-1].start()

    for t in range(3):
        for h in range(HEADS):
            cols = slice(h * HEAD, (h + 1) * HEAD)
            tg_s[t, :, cols] = back[h, 1 + t, :TXT, :]
            ig_s[t, :, cols] = back[h, 1 + t, TXT:, :]
        send(ig_s.at[t], ig.at[t])
        send(tg_s.at[t], tg.at[t])
    for h in range(HEADS):
        cols = slice(h * HEAD, (h + 1) * HEAD)
        ta_s[:, cols] = back[h, 0, :TXT, :]
        io_s[:, cols] = (
            back[h, 0, TXT:, :].astype(jnp.float32)
            + gain[0:1, cols] * residual[:, cols].astype(jnp.float32)
        ).astype(jnp.bfloat16)
    send(io_s, io)
    send(ta_s, ta)
    for copy in copies:
        copy.wait()


def call(kernel, ins, outs, scratch=(), vmem=8, out_place=VM, **kw):
    return pl.pallas_call(
        kernel,
        in_specs=ins,
        out_specs=[out_place] * len(outs) if len(outs) > 1 else out_place,
        out_shape=[jax.ShapeDtypeStruct(s, d) for s, d in outs]
        if len(outs) > 1
        else jax.ShapeDtypeStruct(*outs[0]),
        scratch_shapes=scratch,
        compiler_params=pltpu.CompilerParams(vmem_limit_bytes=vmem << 20),
        **kw,
    )


def body(th, ih, tc, ic, residual, gain, lengths):
    bf16, f32 = jnp.bfloat16, jnp.float32
    chips = ("x", "yl")
    grp = ("yh", "z")
    width = HEADS * HEAD
    core = lax.axis_index("core")
    index = [core, lax.axis_index("yh"), lax.axis_index("z")]
    info = jnp.stack([lengths[0]] + [i.astype(jnp.int32) for i in index])
    send = call(
        pack_kernel,
        [HBM] * 4,
        [((HEADS, 4, ROWS, HEAD), bf16)],
        out_place=HBM,
        scratch=[
            pltpu.VMEM((3, TXT, width), bf16),
            pltpu.VMEM((3, IMG, width), bf16),
            pltpu.VMEM((TXT, width), bf16),
            pltpu.VMEM((IMG, width), bf16),
            pltpu.VMEM((4, HEADS, ROWS, HEAD), bf16),
            pltpu.SemaphoreType.DMA((4, 2)),
            pltpu.SemaphoreType.DMA((4,)),
        ],
        vmem=63,
        name="pack",
    )(jnp.swapaxes(th[0], 0, 1), jnp.swapaxes(ih[0], 0, 1), tc[0], ic[0])
    send, late_ic = lax.optimization_barrier((send, ic[0]))
    own = lax.all_to_all(send, chips, split_axis=0, concat_axis=0, tiled=True)
    swap = [(0, 1), (1, 0)]
    piece = (2, 2, 4, width)
    pieces = call(
        control_pack_kernel,
        [SM] + [VM] * 3,
        [(piece, bf16)] * ZS,
        [pltpu.VMEM((16, 4, width), bf16)],
        name="control_pack",
    )(info, residual[:, 0], late_ic, gain[None, :])

    def shift(x, k):
        return lax.ppermute(x, "z", [(i, (i + k) % ZS) for i in range(ZS)])

    pieces = list(pieces)
    near = pieces[:1] + [shift(pieces[k], k) for k in range(1, EARLY)]
    own, *near = lax.optimization_barrier([own] + near)
    oth = lax.ppermute(own, "core", swap)
    far = lax.ppermute(jnp.stack([p[1] for p in near + pieces[EARLY:]]), "yh", swap)
    def attend(info, own, oth):
        square = ((NQ, NQ), bf16)
        turned = ((2, HEAD, NQ), bf16)
        part, give, e_own, ds_own, qgt = call(
            attention_kernel,
            [SM, VM, VM],
            [((CHIPS, 4, ROWS, HEAD), bf16), turned, square, square, turned],
            [
                pltpu.VMEM((NQ, HEAD), bf16),
                pltpu.VMEM((NQ, HEAD), bf16),
                pltpu.VMEM((NK, HEAD), bf16),
                pltpu.VMEM((NK, HEAD), bf16),
                pltpu.VMEM((BQ, NK), f32),
                pltpu.VMEM((NQ, NQ), bf16),
                pltpu.VMEM((NQ, NQ), bf16),
                pltpu.VMEM((2, 8, HALF_TXT), f32),
            ],
            vmem=32,
            name="attention",
            cost_estimate=pl.CostEstimate(
                flops=12 * NQ * NK * HEAD, bytes_accessed=8 << 20, transcendentals=NQ * NK
            ),
        )(info, own, oth)
        theirs = lax.ppermute(give, "core", swap)
        mine = call(key_grad_kernel, [VM] * 3, [((2, HEAD, NQ), f32)], vmem=16, name="key_grad")(
            qgt, e_own, ds_own
        )
        return call(
            combine_kernel,
            [ANY, VM, VM],
            [((CHIPS, 4, ROWS, HEAD), bf16)],
            out_place=ANY,
            scratch=[pltpu.VMEM((2, CHIPS, ROWS, HEAD), bf16), pltpu.SemaphoreType.DMA((2,))],
            input_output_aliases={0: 0},
            name="combine",
        )(part, mine, theirs)

    ready = lax.cond(
        lengths[0] >= 0,
        attend,
        lambda info, own, oth: jnp.zeros((CHIPS, 4, ROWS, HEAD), bf16),
        info,
        own,
        oth,
    )
    ready, far = lax.optimization_barrier((ready, far))
    late = [jnp.stack([pieces[k][0], far[k]]) for k in range(EARLY, ZS)]
    ready, *late = lax.optimization_barrier([ready] + late)
    late = [shift(x, EARLY + n) for n, x in enumerate(late)]
    back = lax.all_to_all(ready, chips, split_axis=0, concat_axis=0, tiled=True)
    grads, arrived = call(
        control_unpack_kernel,
        [SM] + [VM] * (ZS + 1),
        [((16, 4, width), bf16), ((IMG, width), bf16)],
        [pltpu.VMEM((16, 4, width), bf16)],
        name="control_unpack",
    )(info, *near, far, *late)
    results = [((TXT, width), bf16), ((IMG, width), bf16)]
    results += [((3, TXT, width), bf16), ((3, IMG, width), bf16)]
    ta, io, tg, ig = call(
        unpack_kernel,
        [VM] * 3,
        results,
        out_place=HBM,
        scratch=[pltpu.VMEM(*r) for r in results] + [pltpu.SemaphoreType.DMA((8,))],
        name="unpack",
    )(back, arrived, gain[None, :])
    return (
        ta[None],
        io[None],
        jnp.swapaxes(tg, 0, 1)[None],
        jnp.swapaxes(ig, 0, 1)[None],
        grads[:, None],
    )


def solution(mesh):
    fine = Mesh(mesh.devices.reshape(2, 8, 4, 4, 2), ("yh", "z", "x", "yl", "core"))
    grp = ("yh", "z")
    seq = ("x", "yl", "core")
    in_specs = (
        P(grp, seq, None, None),
        P(grp, seq, None, None),
        P(grp, seq, None),
        P(grp, seq, None),
        P(None, seq, grp, None),
        P(),
        P(grp),
    )
    out_specs = (
        P(grp, seq, None),
        P(grp, seq, None),
        P(grp, seq, None, None),
        P(grp, seq, None, None),
        P(None, seq, grp, None),
    )
    return jax.shard_map(body, mesh=fine, in_specs=in_specs, out_specs=out_specs, check_vma=False)
```

```python
import functools
import math

import jax
import jax.numpy as jnp
from jax import lax
from jax.experimental import pallas as pl
from jax.experimental.pallas import tpu as pltpu
from jax.sharding import Mesh, PartitionSpec as P

HEAD = 128
HEADS = 16
TXT = 16
IMG = 64
ROWS = TXT + IMG
ZS = 8
EARLY = 5
CHIPS = 16
SCALE = 1.0 / math.sqrt(HEAD)
SCALE2 = SCALE * math.log2(math.e)
BQ = 256
NQ = CHIPS * ROWS
NK = 2 * NQ
HALF_TXT = CHIPS * TXT

VM = pl.BlockSpec(memory_space=pltpu.VMEM)
SM = pl.BlockSpec(memory_space=pltpu.SMEM)
ANY = pl.BlockSpec(memory_space=pl.ANY)
HBM = pl.BlockSpec(memory_space=pltpu.HBM)


def dot(a, b):
    return lax.dot_general(a, b, (((1,), (0,)), ((), ())), preferred_element_type=jnp.float32)


def dot_t(a, b):
    return lax.dot_general(a, b, (((1,), (1,)), ((), ())), preferred_element_type=jnp.float32)


def pack_kernel(th, ih, tc, ic, out, th_s, ih_s, tc_s, ic_s, out_s, in_sems, out_sems):
    pairs = [(ih.at[t], ih_s.at[t], th.at[t], th_s.at[t]) for t in range(3)]
    pairs.append((ic, ic_s, tc, tc_s))
    copies = []
    for n, (a, b, c, d) in enumerate(pairs):
        copies.append(
            (
                pltpu.make_async_copy(a, b, in_sems.at[n, 0]),
                pltpu.make_async_copy(c, d, in_sems.at[n, 1]),
            )
        )
    for image, text in copies:
        image.start()
        text.start()
    leaving = []
    for t, (image, text) in enumerate(copies):
        image.wait()
        text.wait()
        for h in range(HEADS):
            cols = slice(h * HEAD, (h + 1) * HEAD)
            out_s[t, h, :TXT, :] = th_s[t, :, cols] if t < 3 else tc_s[:, cols]
            out_s[t, h, TXT:, :] = ih_s[t, :, cols] if t < 3 else ic_s[:, cols]
        leaving.append(pltpu.make_async_copy(out_s.at[t], out.at[:, t], out_sems.at[t]))
        leaving[-1].start()
    for copy in leaving:
        copy.wait()


def control_pack_kernel(info, residual, ic, gain, *refs):
    outs, scaled = refs[:ZS], refs[ZS]
    yh, z = info[2], info[3]
    for r in range(IMG // 16):
        x = ic[r * 16 : (r + 1) * 16, :].astype(jnp.float32) * gain[0:1, :]
        for i in range(4):
            scaled[r * 4 + i] = x[i * 4 : (i + 1) * 4].astype(jnp.bfloat16)
    for k in range(ZS):
        for rel in range(2):
            g = (yh if rel == 0 else 1 - yh) * ZS + lax.rem(z + k, ZS)
            outs[k][rel, 0] = residual[g]
            outs[k][rel, 1] = scaled[g]


def control_unpack_kernel(info, *refs):
    near, far, late = refs[:EARLY], refs[EARLY], refs[EARLY + 1 : ZS + 1]
    grads, arrived, rows = refs[ZS + 1 :]
    yh, z = info[2], info[3]
    for k in range(ZS):
        for rel in range(2):
            g = (yh if rel == 0 else 1 - yh) * ZS + lax.rem(z + ZS - k, ZS)
            if k >= EARLY:
                src = late[k - EARLY].at[rel]
            else:
                src = near[k].at[0] if rel == 0 else far.at[k]
            rows[g] = src[0]
            grads[g] = src[1]
    for r in range(IMG // 16):
        part = [rows[r * 4 + i].astype(jnp.float32) for i in range(4)]
        arrived[r * 16 : (r + 1) * 16, :] = jnp.concatenate(part, axis=0).astype(jnp.bfloat16)


def attention_kernel(
    info, own, oth, aq, give, e_own, ds_own, qgt, q_s, g_s, k_s, v_s, s_s, e_oth, ds_oth, mask_s
):
    length = info[0]
    core = info[1]
    for s in range(CHIPS):
        q_s[s * ROWS : (s + 1) * ROWS, :] = own[s, 0]
        g_s[s * ROWS : (s + 1) * ROWS, :] = own[s, 3]
        for h, src in ((0, own), (1, oth)):
            for t, dst in ((1, k_s), (2, v_s)):
                at = h * NQ + s * TXT
                dst[at : at + TXT, :] = src[s, t, :TXT, :]
                at = h * NQ + HALF_TXT + s * IMG
                dst[at : at + IMG, :] = src[s, t, TXT:, :]
    pos = lax.broadcasted_iota(jnp.int32, (8, HALF_TXT), 1)
    for h in range(2):
        first = (core if h == 0 else 1 - core) * TXT
        token = (pos // TXT) * (2 * TXT) + first + pos % TXT
        mask_s[h] = jnp.where(token < length, 0.0, -jnp.inf)

    def place(i, t, x):
        at, end = i * BQ, (i + 1) * BQ
        while at < end:
            s, r = divmod(at, ROWS)
            n = min(ROWS - r, end - at)
            aq[t, s, r : r + n, :] = x[at - i * BQ : at - i * BQ + n]
            at += n

    def block(i):
        rows = slice(i * BQ, (i + 1) * BQ)
        q = q_s[rows, :]
        g = g_s[rows, :]
        top = None
        for h in range(2):
            s = dot_t(q, k_s[h * NQ : (h + 1) * NQ, :])
            text = s[:, :HALF_TXT] + mask_s[h, 0:1, :]
            s_s[:, h * NQ : h * NQ + HALF_TXT] = text
            s_s[:, h * NQ + HALF_TXT : (h + 1) * NQ] = s[:, HALF_TXT:]
            for t in range(NQ // 128):
                x = (text if t < HALF_TXT // 128 else s)[:, t * 128 : (t + 1) * 128]
                top = x if top is None else jnp.maximum(top, x)
        row_max = jnp.max(top, axis=1, keepdims=True)
        a = total = None
        for h, dst in ((0, e_own), (1, e_oth)):
            cols = slice(h * NQ, (h + 1) * NQ)
            e = jnp.exp2((s_s[:, cols] - row_max) * SCALE2)
            for t in range(NQ // 128):
                x = e[:, t * 128 : (t + 1) * 128]
                total = x if total is None else total + x
            e = e.astype(jnp.bfloat16)
            dst[rows, :] = e
            x = dot(e, v_s[cols, :])
            a = x if a is None else a + x
        inv = 1.0 / jnp.sum(total, axis=1, keepdims=True)
        ab = (a * inv).astype(jnp.bfloat16)
        gs = (g.astype(jnp.float32) * inv).astype(jnp.bfloat16)
        delta = jnp.sum(gs.astype(jnp.float32) * ab.astype(jnp.float32), axis=1, keepdims=True)
        place(i, 0, ab)
        qgt[0, :, rows] = q.T
        qgt[1, :, rows] = gs.T
        dq = None
        for h, src, dst in ((0, e_own, ds_own), (1, e_oth, ds_oth)):
            cols = slice(h * NQ, (h + 1) * NQ)
            dp = dot_t(gs, v_s[cols, :]) - delta
            ds = src[rows, :] * dp.astype(jnp.bfloat16)
            dst[rows, :] = ds
            x = dot(ds, k_s[cols, :])
            dq = x if dq is None else dq + x
        place(i, 1, (dq * SCALE).astype(jnp.bfloat16))

    for i in range(NQ // BQ):
        block(i)
    give[0] = (dot(qgt[0], ds_oth[...]) * SCALE).astype(jnp.bfloat16)
    give[1] = dot(qgt[1], e_oth[...]).astype(jnp.bfloat16)


def key_grad_kernel(qgt, e_own, ds_own, aq, mine, out, sems):
    copies = [pltpu.make_async_copy(aq.at[t], out.at[:, t], sems.at[t]) for t in range(2)]
    for copy in copies:
        copy.start()
    mine[0] = dot(qgt[0], ds_own[...]) * SCALE
    mine[1] = dot(qgt[1], e_own[...])
    for copy in copies:
        copy.wait()


def combine_kernel(part, mine, theirs, out, x_s, sems):
    del part
    copies = []
    for t in range(2):
        x = (mine[t] + theirs[t].astype(jnp.float32)).astype(jnp.bfloat16).T
        for s in range(CHIPS):
            x_s[t, s, :TXT, :] = x[s * TXT : (s + 1) * TXT]
            x_s[t, s, TXT:, :] = x[HALF_TXT + s * IMG : HALF_TXT + (s + 1) * IMG]
        copies.append(pltpu.make_async_copy(x_s.at[t], out.at[:, 2 + t], sems.at[t]))
        copies[-1].start()
    for copy in copies:
        copy.wait()


def unpack_kernel(back, residual, gain, ta, io, tg, ig, ta_s, io_s, tg_s, ig_s, sems):
    copies = []

    def send(a, b):
        copies.append(pltpu.make_async_copy(a, b, sems.at[len(copies)]))
        copies[-1].start()

    for t in range(3):
        for h in range(HEADS):
            cols = slice(h * HEAD, (h + 1) * HEAD)
            tg_s[t, :, cols] = back[h, 1 + t, :TXT, :]
            ig_s[t, :, cols] = back[h, 1 + t, TXT:, :]
        send(ig_s.at[t], ig.at[t])
        send(tg_s.at[t], tg.at[t])
    for h in range(HEADS):
        cols = slice(h * HEAD, (h + 1) * HEAD)
        ta_s[:, cols] = back[h, 0, :TXT, :]
        io_s[:, cols] = (
            back[h, 0, TXT:, :].astype(jnp.float32)
            + gain[0:1, cols] * residual[:, cols].astype(jnp.float32)
        ).astype(jnp.bfloat16)
    send(io_s, io)
    send(ta_s, ta)
    for copy in copies:
        copy.wait()


def call(kernel, ins, outs, scratch=(), vmem=8, out_place=VM, **kw):
    return pl.pallas_call(
        kernel,
        in_specs=ins,
        out_specs=out_place
        if isinstance(out_place, list) or len(outs) == 1
        else [out_place] * len(outs),
        out_shape=[jax.ShapeDtypeStruct(s, d) for s, d in outs]
        if len(outs) > 1
        else jax.ShapeDtypeStruct(*outs[0]),
        scratch_shapes=scratch,
        compiler_params=pltpu.CompilerParams(vmem_limit_bytes=vmem << 20),
        **kw,
    )


def body(th, ih, tc, ic, residual, gain, lengths):
    bf16, f32 = jnp.bfloat16, jnp.float32
    chips = ("x", "yl")
    grp = ("yh", "z")
    width = HEADS * HEAD
    core = lax.axis_index("core")
    index = [core, lax.axis_index("yh"), lax.axis_index("z")]
    info = jnp.stack([lengths[0]] + [i.astype(jnp.int32) for i in index])
    send = call(
        pack_kernel,
        [HBM] * 4,
        [((HEADS, 4, ROWS, HEAD), bf16)],
        out_place=HBM,
        scratch=[
            pltpu.VMEM((3, TXT, width), bf16),
            pltpu.VMEM((3, IMG, width), bf16),
            pltpu.VMEM((TXT, width), bf16),
            pltpu.VMEM((IMG, width), bf16),
            pltpu.VMEM((4, HEADS, ROWS, HEAD), bf16),
            pltpu.SemaphoreType.DMA((4, 2)),
            pltpu.SemaphoreType.DMA((4,)),
        ],
        vmem=63,
        name="pack",
    )(jnp.swapaxes(th[0], 0, 1), jnp.swapaxes(ih[0], 0, 1), tc[0], ic[0])
    send, late_ic = lax.optimization_barrier((send, ic[0]))
    own = lax.all_to_all(send, chips, split_axis=0, concat_axis=0, tiled=True)
    swap = [(0, 1), (1, 0)]
    piece = (2, 2, 4, width)
    pieces = call(
        control_pack_kernel,
        [SM] + [VM] * 3,
        [(piece, bf16)] * ZS,
        [pltpu.VMEM((16, 4, width), bf16)],
        name="control_pack",
    )(info, residual[:, 0], late_ic, gain[None, :])

    def shift(x, k):
        return lax.ppermute(x, "z", [(i, (i + k) % ZS) for i in range(ZS)])

    pieces = list(pieces)
    near = pieces[:1] + [shift(pieces[k], k) for k in range(1, EARLY)]
    own, *near = lax.optimization_barrier([own] + near)
    oth = lax.ppermute(own, "core", swap)
    far = lax.ppermute(jnp.stack([p[1] for p in near + pieces[EARLY:]]), "yh", swap)
    def attend(info, own, oth):
        square = ((NQ, NQ), bf16)
        turned = ((2, HEAD, NQ), bf16)
        aq, give, e_own, ds_own, qgt = call(
            attention_kernel,
            [SM, VM, VM],
            [((2, CHIPS, ROWS, HEAD), bf16), turned, square, square, turned],
            [
                pltpu.VMEM((NQ, HEAD), bf16),
                pltpu.VMEM((NQ, HEAD), bf16),
                pltpu.VMEM((NK, HEAD), bf16),
                pltpu.VMEM((NK, HEAD), bf16),
                pltpu.VMEM((BQ, NK), f32),
                pltpu.VMEM((NQ, NQ), bf16),
                pltpu.VMEM((NQ, NQ), bf16),
                pltpu.VMEM((2, 8, HALF_TXT), f32),
            ],
            vmem=32,
            name="attention",
            cost_estimate=pl.CostEstimate(
                flops=12 * NQ * NK * HEAD, bytes_accessed=8 << 20, transcendentals=NQ * NK
            ),
        )(info, own, oth)
        theirs = lax.ppermute(give, "core", swap)
        mine, part = call(
            key_grad_kernel,
            [VM] * 4,
            [((2, HEAD, NQ), f32), ((CHIPS, 4, ROWS, HEAD), bf16)],
            [pltpu.SemaphoreType.DMA((2,))],
            vmem=16,
            out_place=[VM, ANY],
            name="key_grad",
        )(qgt, e_own, ds_own, aq)
        return call(
            combine_kernel,
            [ANY, VM, VM],
            [((CHIPS, 4, ROWS, HEAD), bf16)],
            out_place=ANY,
            scratch=[pltpu.VMEM((2, CHIPS, ROWS, HEAD), bf16), pltpu.SemaphoreType.DMA((2,))],
            input_output_aliases={0: 0},
            name="combine",
        )(part, mine, theirs)

    ready = lax.cond(
        lengths[0] >= 0,
        attend,
        lambda info, own, oth: jnp.zeros((CHIPS, 4, ROWS, HEAD), bf16),
        info,
        own,
        oth,
    )
    ready, far = lax.optimization_barrier((ready, far))
    late = [jnp.stack([pieces[k][0], far[k]]) for k in range(EARLY, ZS)]
    ready, *late = lax.optimization_barrier([ready] + late)
    late = [shift(x, EARLY + n) for n, x in enumerate(late)]
    back = lax.all_to_all(ready, chips, split_axis=0, concat_axis=0, tiled=True)
    grads, arrived = call(
        control_unpack_kernel,
        [SM] + [VM] * (ZS + 1),
        [((16, 4, width), bf16), ((IMG, width), bf16)],
        [pltpu.VMEM((16, 4, width), bf16)],
        name="control_unpack",
    )(info, *near, far, *late)
    results = [((TXT, width), bf16), ((IMG, width), bf16)]
    results += [((3, TXT, width), bf16), ((3, IMG, width), bf16)]
    ta, io, tg, ig = call(
        unpack_kernel,
        [VM] * 3,
        results,
        out_place=HBM,
        scratch=[pltpu.VMEM(*r) for r in results] + [pltpu.SemaphoreType.DMA((8,))],
        name="unpack",
    )(back, arrived, gain[None, :])
    return (
        ta[None],
        io[None],
        jnp.swapaxes(tg, 0, 1)[None],
        jnp.swapaxes(ig, 0, 1)[None],
        grads[:, None],
    )


def solution(mesh):
    fine = Mesh(mesh.devices.reshape(2, 8, 4, 4, 2), ("yh", "z", "x", "yl", "core"))
    grp = ("yh", "z")
    seq = ("x", "yl", "core")
    in_specs = (
        P(grp, seq, None, None),
        P(grp, seq, None, None),
        P(grp, seq, None),
        P(grp, seq, None),
        P(None, seq, grp, None),
        P(),
        P(grp),
    )
    out_specs = (
        P(grp, seq, None),
        P(grp, seq, None),
        P(grp, seq, None, None),
        P(grp, seq, None, None),
        P(None, seq, grp, None),
    )
    return jax.shard_map(body, mesh=fine, in_specs=in_specs, out_specs=out_specs, check_vma=False)
```

```python
import functools
import math

import jax
import jax.numpy as jnp
from jax import lax
from jax.experimental import pallas as pl
from jax.experimental.pallas import tpu as pltpu
from jax.sharding import Mesh, PartitionSpec as P

HEAD = 128
HEADS = 16
TXT = 16
IMG = 64
ROWS = TXT + IMG
ZS = 8
EARLY = 5
CHIPS = 16
SCALE = 1.0 / math.sqrt(HEAD)
SCALE2 = SCALE * math.log2(math.e)
BQ = 256
NQ = CHIPS * ROWS
NK = 2 * NQ
HALF_TXT = CHIPS * TXT

VM = pl.BlockSpec(memory_space=pltpu.VMEM)
SM = pl.BlockSpec(memory_space=pltpu.SMEM)
ANY = pl.BlockSpec(memory_space=pl.ANY)
HBM = pl.BlockSpec(memory_space=pltpu.HBM)


def dot(a, b):
    return lax.dot_general(a, b, (((1,), (0,)), ((), ())), preferred_element_type=jnp.float32)


def dot_t(a, b):
    return lax.dot_general(a, b, (((1,), (1,)), ((), ())), preferred_element_type=jnp.float32)


def pack_kernel(th, ih, tc, ic, out, th_s, ih_s, tc_s, ic_s, out_s, in_sems, out_sems):
    pairs = [(ih.at[t], ih_s.at[t], th.at[t], th_s.at[t]) for t in range(3)]
    pairs.append((ic, ic_s, tc, tc_s))
    copies = []
    for n, (a, b, c, d) in enumerate(pairs):
        copies.append(
            (
                pltpu.make_async_copy(a, b, in_sems.at[n, 0]),
                pltpu.make_async_copy(c, d, in_sems.at[n, 1]),
            )
        )
    for image, text in copies:
        image.start()
        text.start()
    leaving = []
    for t, (image, text) in enumerate(copies):
        image.wait()
        text.wait()
        for h in range(HEADS):
            cols = slice(h * HEAD, (h + 1) * HEAD)
            out_s[t, h, :TXT, :] = th_s[t, :, cols] if t < 3 else tc_s[:, cols]
            out_s[t, h, TXT:, :] = ih_s[t, :, cols] if t < 3 else ic_s[:, cols]
        leaving.append(pltpu.make_async_copy(out_s.at[t], out.at[:, t], out_sems.at[t]))
        leaving[-1].start()
    for copy in leaving:
        copy.wait()


def control_pack_kernel(info, residual, ic, gain, *refs):
    outs, scaled = refs[:ZS], refs[ZS]
    yh, z = info[2], info[3]
    for r in range(IMG // 16):
        x = ic[r * 16 : (r + 1) * 16, :].astype(jnp.float32) * gain[0:1, :]
        for i in range(4):
            scaled[r * 4 + i] = x[i * 4 : (i + 1) * 4].astype(jnp.bfloat16)
    for k in range(ZS):
        for rel in range(2):
            g = (yh if rel == 0 else 1 - yh) * ZS + lax.rem(z + k, ZS)
            outs[k][rel, 0] = residual[g]
            outs[k][rel, 1] = scaled[g]


def control_unpack_kernel(info, *refs):
    near, far, late = refs[:EARLY], refs[EARLY], refs[EARLY + 1 : ZS + 1]
    grads, arrived, rows = refs[ZS + 1 :]
    yh, z = info[2], info[3]
    for k in range(ZS):
        for rel in range(2):
            g = (yh if rel == 0 else 1 - yh) * ZS + lax.rem(z + ZS - k, ZS)
            if k >= EARLY:
                src = late[k - EARLY].at[rel]
            else:
                src = near[k].at[0] if rel == 0 else far.at[k]
            rows[g] = src[0]
            grads[g] = src[1]
    for r in range(IMG // 16):
        part = [rows[r * 4 + i].astype(jnp.float32) for i in range(4)]
        arrived[r * 16 : (r + 1) * 16, :] = jnp.concatenate(part, axis=0).astype(jnp.bfloat16)


def attention_kernel(
    info, own, oth, aq, give, e_own, ds_own, qgt, q_s, g_s, k_s, v_s, s_s, e_oth, ds_oth, mask_s
):
    length = info[0]
    core = info[1]
    for s in range(CHIPS):
        q_s[s * ROWS : (s + 1) * ROWS, :] = own[s, 0]
        g_s[s * ROWS : (s + 1) * ROWS, :] = own[s, 3]
        for h, src in ((0, own), (1, oth)):
            for t, dst in ((1, k_s), (2, v_s)):
                at = h * NQ + s * TXT
                dst[at : at + TXT, :] = src[s, t, :TXT, :]
                at = h * NQ + HALF_TXT + s * IMG
                dst[at : at + IMG, :] = src[s, t, TXT:, :]
    pos = lax.broadcasted_iota(jnp.int32, (8, HALF_TXT), 1)
    for h in range(2):
        first = (core if h == 0 else 1 - core) * TXT
        token = (pos // TXT) * (2 * TXT) + first + pos % TXT
        mask_s[h] = jnp.where(token < length, 0.0, -jnp.inf)

    def place(i, t, x):
        at, end = i * BQ, (i + 1) * BQ
        while at < end:
            s, r = divmod(at, ROWS)
            n = min(ROWS - r, end - at)
            aq[t, s, r : r + n, :] = x[at - i * BQ : at - i * BQ + n]
            at += n

    def block(i):
        rows = slice(i * BQ, (i + 1) * BQ)
        q = q_s[rows, :]
        g = g_s[rows, :]
        top = None
        for h in range(2):
            s = dot_t(q, k_s[h * NQ : (h + 1) * NQ, :])
            text = s[:, :HALF_TXT] + mask_s[h, 0:1, :]
            s_s[:, h * NQ : h * NQ + HALF_TXT] = text
            s_s[:, h * NQ + HALF_TXT : (h + 1) * NQ] = s[:, HALF_TXT:]
            for t in range(NQ // 128):
                x = (text if t < HALF_TXT // 128 else s)[:, t * 128 : (t + 1) * 128]
                top = x if top is None else jnp.maximum(top, x)
        row_max = jnp.max(top, axis=1, keepdims=True)
        a = total = None
        for h, dst in ((0, e_own), (1, e_oth)):
            cols = slice(h * NQ, (h + 1) * NQ)
            e = jnp.exp2((s_s[:, cols] - row_max) * SCALE2)
            for t in range(NQ // 128):
                x = e[:, t * 128 : (t + 1) * 128]
                total = x if total is None else total + x
            e = e.astype(jnp.bfloat16)
            dst[rows, :] = e
            x = dot(e, v_s[cols, :])
            a = x if a is None else a + x
        inv = 1.0 / jnp.sum(total, axis=1, keepdims=True)
        ab = (a * inv).astype(jnp.bfloat16)
        gs = (g.astype(jnp.float32) * inv).astype(jnp.bfloat16)
        delta = jnp.sum(gs.astype(jnp.float32) * ab.astype(jnp.float32), axis=1, keepdims=True)
        place(i, 0, ab)
        qgt[0, :, rows] = q.T
        qgt[1, :, rows] = gs.T
        dq = None
        for h, src, dst in ((0, e_own, ds_own), (1, e_oth, ds_oth)):
            cols = slice(h * NQ, (h + 1) * NQ)
            dp = dot_t(gs, v_s[cols, :]) - delta
            ds = src[rows, :] * dp.astype(jnp.bfloat16)
            dst[rows, :] = ds
            x = dot(ds, k_s[cols, :])
            dq = x if dq is None else dq + x
        place(i, 1, (dq * SCALE).astype(jnp.bfloat16))

    for i in range(NQ // BQ):
        block(i)
    give[0] = (dot(qgt[0], ds_oth[...]) * SCALE).astype(jnp.bfloat16)
    give[1] = dot(qgt[1], e_oth[...]).astype(jnp.bfloat16)


def key_grad_kernel(qgt, e_own, ds_own, aq, mine, out, sems):
    copies = [pltpu.make_async_copy(aq.at[t], out.at[:, t], sems.at[t]) for t in range(2)]
    for copy in copies:
        copy.start()
    mine[0] = dot(qgt[0], ds_own[...]) * SCALE
    mine[1] = dot(qgt[1], e_own[...])
    for copy in copies:
        copy.wait()


def combine_kernel(part, mine, theirs, out, x_s, sems):
    del part
    copies = []
    for t in range(2):
        x = (mine[t] + theirs[t].astype(jnp.float32)).astype(jnp.bfloat16).T
        for s in range(CHIPS):
            x_s[t, s, :TXT, :] = x[s * TXT : (s + 1) * TXT]
            x_s[t, s, TXT:, :] = x[HALF_TXT + s * IMG : HALF_TXT + (s + 1) * IMG]
        copies.append(pltpu.make_async_copy(x_s.at[t], out.at[:, 2 + t], sems.at[t]))
        copies[-1].start()
    for copy in copies:
        copy.wait()


def unpack_kernel(back, residual, gain, ta, io, tg, ig, ta_s, io_s, tg_s, ig_s, sems):
    copies = []

    def send(a, b):
        copies.append(pltpu.make_async_copy(a, b, sems.at[len(copies)]))
        copies[-1].start()

    for h in range(HEADS):
        cols = slice(h * HEAD, (h + 1) * HEAD)
        ta_s[:, cols] = back[h, 0, :TXT, :]
        io_s[:, cols] = (
            back[h, 0, TXT:, :].astype(jnp.float32)
            + gain[0:1, cols] * residual[:, cols].astype(jnp.float32)
        ).astype(jnp.bfloat16)
    send(io_s, io)
    send(ta_s, ta)
    for t in range(3):
        for h in range(HEADS):
            cols = slice(h * HEAD, (h + 1) * HEAD)
            tg_s[t, :, cols] = back[h, 1 + t, :TXT, :]
            ig_s[t, :, cols] = back[h, 1 + t, TXT:, :]
        send(ig_s.at[t], ig.at[t])
        send(tg_s.at[t], tg.at[t])
    for copy in copies:
        copy.wait()


def call(kernel, ins, outs, scratch=(), vmem=8, out_place=VM, **kw):
    return pl.pallas_call(
        kernel,
        in_specs=ins,
        out_specs=out_place
        if isinstance(out_place, list) or len(outs) == 1
        else [out_place] * len(outs),
        out_shape=[jax.ShapeDtypeStruct(s, d) for s, d in outs]
        if len(outs) > 1
        else jax.ShapeDtypeStruct(*outs[0]),
        scratch_shapes=scratch,
        compiler_params=pltpu.CompilerParams(vmem_limit_bytes=vmem << 20),
        **kw,
    )


def body(th, ih, tc, ic, residual, gain, lengths):
    bf16, f32 = jnp.bfloat16, jnp.float32
    chips = ("x", "yl")
    grp = ("yh", "z")
    width = HEADS * HEAD
    core = lax.axis_index("core")
    index = [core, lax.axis_index("yh"), lax.axis_index("z")]
    info = jnp.stack([lengths[0]] + [i.astype(jnp.int32) for i in index])
    send = call(
        pack_kernel,
        [HBM] * 4,
        [((HEADS, 4, ROWS, HEAD), bf16)],
        out_place=HBM,
        scratch=[
            pltpu.VMEM((3, TXT, width), bf16),
            pltpu.VMEM((3, IMG, width), bf16),
            pltpu.VMEM((TXT, width), bf16),
            pltpu.VMEM((IMG, width), bf16),
            pltpu.VMEM((4, HEADS, ROWS, HEAD), bf16),
            pltpu.SemaphoreType.DMA((4, 2)),
            pltpu.SemaphoreType.DMA((4,)),
        ],
        vmem=63,
        name="pack",
    )(jnp.swapaxes(th[0], 0, 1), jnp.swapaxes(ih[0], 0, 1), tc[0], ic[0])
    send, late_ic = lax.optimization_barrier((send, ic[0]))
    own = lax.all_to_all(send, chips, split_axis=0, concat_axis=0, tiled=True)
    swap = [(0, 1), (1, 0)]
    piece = (2, 2, 4, width)
    pieces = call(
        control_pack_kernel,
        [SM] + [VM] * 3,
        [(piece, bf16)] * ZS,
        [pltpu.VMEM((16, 4, width), bf16)],
        name="control_pack",
    )(info, residual[:, 0], late_ic, gain[None, :])

    def shift(x, k):
        return lax.ppermute(x, "z", [(i, (i + k) % ZS) for i in range(ZS)])

    pieces = list(pieces)
    near = pieces[:1] + [shift(pieces[k], k) for k in range(1, EARLY)]
    own, *near = lax.optimization_barrier([own] + near)
    oth = lax.ppermute(own, "core", swap)
    far = lax.ppermute(jnp.stack([p[1] for p in near + pieces[EARLY:]]), "yh", swap)
    def attend(info, own, oth):
        square = ((NQ, NQ), bf16)
        turned = ((2, HEAD, NQ), bf16)
        aq, give, e_own, ds_own, qgt = call(
            attention_kernel,
            [SM, VM, VM],
            [((2, CHIPS, ROWS, HEAD), bf16), turned, square, square, turned],
            [
                pltpu.VMEM((NQ, HEAD), bf16),
                pltpu.VMEM((NQ, HEAD), bf16),
                pltpu.VMEM((NK, HEAD), bf16),
                pltpu.VMEM((NK, HEAD), bf16),
                pltpu.VMEM((BQ, NK), f32),
                pltpu.VMEM((NQ, NQ), bf16),
                pltpu.VMEM((NQ, NQ), bf16),
                pltpu.VMEM((2, 8, HALF_TXT), f32),
            ],
            vmem=32,
            name="attention",
            cost_estimate=pl.CostEstimate(
                flops=12 * NQ * NK * HEAD, bytes_accessed=8 << 20, transcendentals=NQ * NK
            ),
        )(info, own, oth)
        theirs = lax.ppermute(give, "core", swap)
        mine, part = call(
            key_grad_kernel,
            [VM] * 4,
            [((2, HEAD, NQ), f32), ((CHIPS, 4, ROWS, HEAD), bf16)],
            [pltpu.SemaphoreType.DMA((2,))],
            vmem=16,
            out_place=[VM, ANY],
            name="key_grad",
        )(qgt, e_own, ds_own, aq)
        return call(
            combine_kernel,
            [ANY, VM, VM],
            [((CHIPS, 4, ROWS, HEAD), bf16)],
            out_place=ANY,
            scratch=[pltpu.VMEM((2, CHIPS, ROWS, HEAD), bf16), pltpu.SemaphoreType.DMA((2,))],
            input_output_aliases={0: 0},
            name="combine",
        )(part, mine, theirs)

    ready = lax.cond(
        lengths[0] >= 0,
        attend,
        lambda info, own, oth: jnp.zeros((CHIPS, 4, ROWS, HEAD), bf16),
        info,
        own,
        oth,
    )
    ready, far = lax.optimization_barrier((ready, far))
    late = [jnp.stack([pieces[k][0], far[k]]) for k in range(EARLY, ZS)]
    ready, *late = lax.optimization_barrier([ready] + late)
    late = [shift(x, EARLY + n) for n, x in enumerate(late)]
    back = lax.all_to_all(ready, chips, split_axis=0, concat_axis=0, tiled=True)
    grads, arrived = call(
        control_unpack_kernel,
        [SM] + [VM] * (ZS + 1),
        [((16, 4, width), bf16), ((IMG, width), bf16)],
        [pltpu.VMEM((16, 4, width), bf16)],
        name="control_unpack",
    )(info, *near, far, *late)
    results = [((TXT, width), bf16), ((IMG, width), bf16)]
    results += [((3, TXT, width), bf16), ((3, IMG, width), bf16)]
    ta, io, tg, ig = call(
        unpack_kernel,
        [VM] * 3,
        results,
        out_place=HBM,
        scratch=[pltpu.VMEM(*r) for r in results] + [pltpu.SemaphoreType.DMA((8,))],
        name="unpack",
    )(back, arrived, gain[None, :])
    return (
        ta[None],
        io[None],
        jnp.swapaxes(tg, 0, 1)[None],
        jnp.swapaxes(ig, 0, 1)[None],
        grads[:, None],
    )


def solution(mesh):
    fine = Mesh(mesh.devices.reshape(2, 8, 4, 4, 2), ("yh", "z", "x", "yl", "core"))
    grp = ("yh", "z")
    seq = ("x", "yl", "core")
    in_specs = (
        P(grp, seq, None, None),
        P(grp, seq, None, None),
        P(grp, seq, None),
        P(grp, seq, None),
        P(None, seq, grp, None),
        P(),
        P(grp),
    )
    out_specs = (
        P(grp, seq, None),
        P(grp, seq, None),
        P(grp, seq, None, None),
        P(grp, seq, None, None),
        P(None, seq, grp, None),
    )
    return jax.shard_map(body, mesh=fine, in_specs=in_specs, out_specs=out_specs, check_vma=False)
```
